32 devices in a mesh: tiles: 2 (over y), band: 4 (over x, core), head: 4 (over z).
Axes of the slice: x: 2, y: 2, z: 4, core: 2. Of those that a mesh axis runs over, the one named last changes fastest.
Arguments:
- tokens: bfloat16 [8192, 1024], P(('tiles', 'band')), parts along dimension 0, may hold values from -24 to 24
- w_query: bfloat16 [1024, 1024], P(None, 'head'), may hold values from -0.375 to 0.375
- w_key: bfloat16 [1024, 1024], P(None, 'head'), may hold values from -0.1875 to 0.1875
- w_value: bfloat16 [1024, 1024], P(None, 'head'), may hold values from -0.1875 to 0.1875
- w_out: bfloat16 [1024, 1024], P('head'), may hold values from -0.75 to 0.75
- block_mask: int32 [64, 32], P('tiles'), parts along dimension 0, may hold values from 0 to 1, as said below
Outputs:
- projected: bfloat16 [8192, 1024], P(('tiles', 'band', 'head')), parts along dimension 0
The draws below stay inside these ranges and needn't reach their ends.
There are 2 independent parts, one for each index of `tiles`. The reference program is written for one: setup_inputs(seed, part) draws one part's arguments, and reference() takes and returns one part's arrays. A program takes and returns all parts, laid end to end along the dimension named above; an argument that names none is the same for every part. Nothing has to cross between parts.
Inputs may be any that keep to these rules, and one draw needn't show every extreme that they name: `block_mask`: entries are 0 or 1. Every query block may attend to at least one key block. Among the 8 key blocks of one band at most 6 are named by some query block, and some band has exactly 6.
All inputs are finite; a program needn't handle non-finite values.
Results may differ from the reference program's by a relative error of at most 0.02.
Values may be sent and summed in bfloat16 or wider, within the bound.
A program may use at most 128 MiB of HBM per device.

```python
import math
import jax
import jax.numpy as jnp
from jax import lax

D = 1024
HEADS = 16
HD = 64
BLK = 128
TOK_DEV = 1024
TOKENS = 4096
KEEP = 6


def draw_tokens(key, part):
    first, second = jax.random.split(key, 2)
    base = jax.random.truncated_normal(first, -4.0, 4.0, (TOKENS, D), jnp.float32)
    row_scale = jnp.exp(jax.random.uniform(second, (TOKENS, 1), jnp.float32, math.log(0.7), math.log(1.4)))
    return (base * row_scale).astype(jnp.bfloat16)


def draw_block_mask(key, part):
    block_total = TOKENS // BLK
    per_band = TOK_DEV // BLK
    band_total = TOKENS // TOK_DEV
    streams = jax.random.split(key, 7)
    lowest = (KEEP + 1) // 2
    kept_counts = jax.random.randint(streams[0], (band_total,), lowest, KEEP + 1)
    forced = jax.random.randint(streams[1], (), 0, band_total)
    kept_counts = jnp.where(jnp.arange(band_total) == forced, KEEP, kept_counts)
    raw_order = jax.random.randint(streams[2], (band_total, per_band), 0, 1 << 20) * per_band + jnp.arange(per_band)[None, :]
    block_ranks = jnp.argsort(jnp.argsort(raw_order, axis=1), axis=1)
    has_data = (block_ranks < kept_counts[:, None]).reshape(block_total).astype(jnp.int32)
    levels = jax.random.randint(streams[3], (band_total,), 0, 8)
    percent = 4 + 88 * levels * levels // 49
    band_of_row = jnp.arange(block_total) // per_band
    chance = jax.random.randint(streams[4], (block_total, block_total), 0, 100)
    allowed = (chance < percent[band_of_row][:, None]).astype(jnp.int32) * has_data[None, :]
    pick_raw = (jax.random.randint(streams[5], (block_total, block_total), 0, 1 << 16) * block_total + jnp.arange(block_total)[None, :] + 1) * has_data[None, :]
    picked = jnp.argmax(pick_raw, axis=1)
    allowed = jnp.maximum(allowed, (jnp.arange(block_total)[None, :] == picked[:, None]).astype(jnp.int32))
    row_pick = jax.random.randint(streams[6], (block_total,), 0, block_total)
    column_hits = (jnp.arange(block_total)[:, None] == row_pick[None, :]).astype(jnp.int32) * has_data[None, :]
    allowed = jnp.maximum(allowed, column_hits)
    return allowed.astype(jnp.int32)


def block_levels(stream_key, shape, shards, low, high):
    def one(dim, blocks):
        draws = jax.random.uniform(jax.random.fold_in(jax.random.fold_in(stream_key, 6), dim), (blocks,), jnp.float32, low / len(shards), high / len(shards))
        return jnp.repeat(jnp.exp(draws), shape[dim] // blocks).reshape((-1,) + (1,) * (len(shape) - dim - 1))

    level = one(*shards[0])
    for cut in shards[1:]:
        level = level * one(*cut)
    return level


def scatter_about(rng, dims, width, reach, cuts=(), held_as=jnp.bfloat16):
    level = block_levels(rng, dims, cuts, -0.22, 0.18) if cuts else 1.0
    array = jax.random.normal(rng, dims, jnp.float32) * width * level
    return jnp.minimum(jnp.maximum(array, -reach), reach).astype(held_as)


def setup_inputs(seed: int = 0, part: int = 0) -> dict:
    seeds = jax.random.split(jax.random.key(seed), 7)
    own_keys = jax.random.split(jax.random.fold_in(seeds[6], part), 7)
    return {
        "tokens": draw_tokens(jax.random.fold_in(jax.random.fold_in(seeds[6], part), 71), part),
        "w_query": scatter_about(seeds[1], (D, D), (D // 4) ** -0.5, 0.375, ((1, 4),)),
        "w_key": scatter_about(seeds[2], (D, D), D ** -0.5, 0.1875, ((1, 4),)),
        "w_value": scatter_about(seeds[3], (D, D), D ** -0.5, 0.1875, ((1, 4),)),
        "w_out": scatter_about(seeds[4], (D, D), HD ** -0.5, 0.75, ((0, 4),)),
        "block_mask": draw_block_mask(jax.random.fold_in(jax.random.fold_in(seeds[6], part), 71), part),
    }


def reference(tokens, w_query, w_key, w_value, w_out, block_mask):
    queries = jnp.dot(tokens, w_query, preferred_element_type=jnp.float32).astype(jnp.bfloat16)
    key_rows = jnp.dot(tokens, w_key, preferred_element_type=jnp.float32).astype(jnp.bfloat16)
    value_rows = jnp.dot(tokens, w_value, preferred_element_type=jnp.float32).astype(jnp.bfloat16)
    total_rows = tokens.shape[0]
    block_count = total_rows // BLK
    key_heads = key_rows.astype(jnp.float32).reshape(total_rows, HEADS, HD)
    value_heads = value_rows.astype(jnp.float32).reshape(total_rows, HEADS, HD)
    score_scale = HD ** -0.5

    def one_block(packed):
        query_block, mask_row = packed
        query_heads = query_block.astype(jnp.float32).reshape(BLK, HEADS, HD)
        scores = jnp.einsum("rhd,khd->hrk", query_heads, key_heads, precision=lax.Precision.HIGHEST) * score_scale
        keep_keys = jnp.repeat(mask_row, BLK) > 0
        scores = jnp.where(keep_keys[None, None, :], scores, -jnp.inf)
        row_peak = jnp.max(scores, axis=2, keepdims=True)
        exponent = jnp.where(keep_keys[None, None, :], jnp.exp(scores - row_peak), 0.0)
        row_mass = jnp.sum(exponent, axis=2)
        rounded = lax.optimization_barrier(exponent.astype(jnp.bfloat16)).astype(jnp.float32)
        weighted = jnp.einsum("hrk,khd->rhd", rounded, value_heads, precision=lax.Precision.HIGHEST)
        return (weighted / row_mass.T[:, :, None]).reshape(BLK, HEADS * HD).astype(jnp.bfloat16)

    attended = lax.map(one_block, (queries.reshape(block_count, BLK, HEADS * HD), block_mask))
    attended = attended.reshape(total_rows, HEADS * HD)
    return jnp.dot(attended, w_out, preferred_element_type=jnp.float32).astype(jnp.bfloat16)
```

```python
import functools
import jax
import jax.numpy as jnp
from jax import lax
from jax.experimental import pallas as pl
from jax.experimental.pallas import tpu as pltpu
from jax.sharding import PartitionSpec as P

HD = 64
BLK = 128
KEEP = 6
UNROLL = 4
LOW = -1e30
SCALE = HD**-0.5 * 1.4426950408889634
MIB = 1 << 20
BF16 = jnp.bfloat16
F32 = jnp.float32
NT = (((1,), (1,)), ((), ()))
TN = (((0,), (0,)), ((), ()))


def greet(peers):
    barrier = pltpu.get_barrier_semaphore()
    for peer in peers:
        pl.semaphore_signal(barrier, inc=1, device_id=peer, device_id_type=pl.DeviceIdType.MESH)
    pl.semaphore_wait(barrier, len(peers))


def project_exchange(nb, nh, sel, tok, wq, wk, wv, q_all, kv_all, qs, kvs, send_kv, recv_kv, send_q, recv_q, own):
    me = lax.axis_index("band")
    group, place = me // nh, lax.rem(me, nh)
    nq = tok.shape[0]
    others = [lax.rem(me + d, nb) for d in range(1, nb)]
    greet([{"band": p} for p in others])

    for k in range(KEEP):
        rows = tok[sel[k]]
        keys = jnp.dot(rows, wk[...], preferred_element_type=F32)
        vals = jnp.dot(rows, wv[...], preferred_element_type=F32)
        for h in range(nh):
            cut = slice(h * HD, (h + 1) * HD)
            kvs[h, k] = jnp.concatenate([keys[:, cut], vals[:, cut]], axis=1).astype(BF16)

    def kv_copy(peer, origin):
        return pltpu.make_async_remote_copy(
            src_ref=kvs.at[lax.rem(peer, nh)],
            dst_ref=kv_all.at[pl.ds(origin * KEEP, KEEP)],
            send_sem=send_kv.at[peer],
            recv_sem=recv_kv.at[origin],
            device_id={"band": peer},
            device_id_type=pl.DeviceIdType.MESH,
        )

    order = [p for _, p in sorted(zip([abs(d - nb // 2) for d in range(1, nb)], range(nb - 1)))]
    for i in order:
        kv_copy(others[i], me).start()
    own_kv = pltpu.make_async_copy(kvs.at[place], kv_all.at[pl.ds(me * KEEP, KEEP)], own.at[0])
    own_kv.start()

    for m in range(nq // 2):
        two = jnp.dot(
            jnp.concatenate([tok[2 * m], tok[2 * m + 1]], axis=0), wq[...], preferred_element_type=F32
        )
        for h in range(nh):
            cut = slice(h * HD, (h + 1) * HD)
            qs[h, m] = jnp.concatenate([two[:BLK, cut], two[BLK:, cut]], axis=1).astype(BF16)

    def q_copy(to, origin):
        return pltpu.make_async_remote_copy(
            src_ref=qs.at[to],
            dst_ref=q_all.at[origin],
            send_sem=send_q.at[to],
            recv_sem=recv_q.at[origin],
            device_id={"band": group * nh + to},
            device_id_type=pl.DeviceIdType.MESH,
        )

    mates = [lax.rem(place + d, nh) for d in range(1, nh)]
    order_q = [i for _, i in sorted(zip([abs(d - nh // 2) for d in range(1, nh)], range(nh - 1)))]
    for i in order_q:
        q_copy(mates[i], place).start()
    own_q = pltpu.make_async_copy(qs.at[place], q_all.at[place], own.at[1])
    own_q.start()
    own_kv.wait()
    own_q.wait()
    for p in others:
        kv_copy(p, me).wait_send()
        kv_copy(p, p).wait_recv()
    for p in mates:
        q_copy(p, place).wait_send()
        q_copy(p, p).wait_recv()


def attend(work, turns, q_in, kv, out, q_pad, v_t):
    n_kv, n_pair = kv.shape[0], q_in.shape[0]
    lane = lax.broadcasted_iota(jnp.int32, (BLK, BLK), 1)

    def prepare_kv(c, _):
        v_t[c] = kv[c].T[HD:]
        return 0

    lax.fori_loop(0, n_kv, prepare_kv, 0, unroll=4)

    def prepare_q(m, _):
        two = q_in[m].astype(F32)
        q_pad[2 * m] = jnp.where(lane < HD, two, 0.0).astype(BF16)
        q_pad[2 * m + 1] = jnp.where(lane < HD, pltpu.roll(two, HD, 1), 0.0).astype(BF16)
        return 0

    lax.fori_loop(0, n_pair, prepare_q, 0, unroll=2)
    q_pad[2 * n_pair] = jnp.zeros((BLK, BLK), BF16)

    def turn(i, state):
        peak, mass, total = state
        parts = []
        for u in range(UNROLL):
            t = i * UNROLL + u
            q, a, b = work[0, t], work[1, t], work[2, t]
            scores = lax.dot_general(
                jnp.concatenate([kv[a], kv[b]], axis=0), q_pad[q], NT, preferred_element_type=F32
            ) * SCALE
            bias = jnp.where(work[3, t] > 0, 0.0, LOW)
            scores = jnp.concatenate([scores[:BLK], scores[BLK:] + bias], axis=0)
            top = jnp.max(scores, axis=0, keepdims=True)
            weight = jnp.exp2(scores - top)
            part = jnp.sum(weight, axis=0, keepdims=True)
            values = jnp.concatenate([v_t[a], v_t[b]], axis=1)
            got = jnp.dot(values, weight.astype(BF16), preferred_element_type=F32)
            parts.append((q, work[4, t], top, part, got))
        for q, first, top, part, got in parts:
            before = jnp.where(first > 0, LOW, peak)
            peak = jnp.maximum(before, top)
            f, g = jnp.exp2(before - peak), jnp.exp2(top - peak)
            mass = mass * f + part * g
            total = total * f + got * g
            out[q] = (total / mass).astype(BF16)
        return peak, mass, total

    start = (jnp.full((1, BLK), LOW, F32), jnp.zeros((1, BLK), F32), jnp.zeros((HD, BLK), F32))
    lax.fori_loop(0, turns[0], turn, start)


def exchange_project(nh, nz, att, w_full, out, got, send, recv, own):
    band, z = lax.axis_index("band"), lax.axis_index("head")
    group, place = band // nh, lax.rem(band, nh)
    n = nh * nz
    me = z * nh + place
    per = got.shape[1]
    per_band = per * nz
    others = [lax.rem(me + d, n) for d in range(1, n)]
    where = lambda p: {"band": group * nh + lax.rem(p, nh), "head": p // nh}
    greet([where(p) for p in others])

    def piece(p):
        return att.at[pl.ds(lax.rem(p, nh) * per_band + (p // nh) * per, per)]

    def copy(peer, origin):
        return pltpu.make_async_remote_copy(
            src_ref=piece(peer),
            dst_ref=got.at[origin],
            send_sem=send.at[peer],
            recv_sem=recv.at[origin],
            device_id=where(peer),
            device_id_type=pl.DeviceIdType.MESH,
        )

    for _, i in sorted(zip([abs(d - n // 2) for d in range(1, n)], range(n - 1))):
        copy(others[i], me).start()
    mine = pltpu.make_async_copy(piece(me), got.at[me], own.at[0])
    mine.start()
    mine.wait()
    for p in others:
        copy(p, me).wait_send()
        copy(p, p).wait_recv()
    for r in range(per):
        heads = jnp.concatenate([got[i, r] for i in range(n)], axis=0)
        out[pl.ds(r * BLK, BLK), :] = lax.dot_general(
            heads, w_full[...], TN, preferred_element_type=F32
        ).astype(BF16)


def plan(block_mask, nb, nh, me):
    n_kb = block_mask.shape[1]
    per_band = n_kb // nb
    nq = per_band * nh
    i32 = jnp.int32
    named = jnp.max(block_mask, axis=0).reshape(nb, per_band)
    low = jnp.arange(per_band)[:, None] < jnp.arange(per_band)[None, :]
    rank = jnp.sum(named[:, :, None] * low[None].astype(i32), axis=1)
    place = (jnp.arange(nb, dtype=i32)[:, None] * KEEP + jnp.minimum(rank, KEEP - 1)).reshape(-1)
    hit = (named[:, None, :] > 0) & (rank[:, None, :] == jnp.arange(KEEP)[None, :, None])
    sel_all = jnp.sum(jnp.where(hit, jnp.arange(per_band, dtype=i32)[None, None, :], 0), axis=2)
    sel = lax.dynamic_index_in_dim(sel_all, me, 0, keepdims=False)
    rows = lax.dynamic_slice_in_dim(block_mask, (me // nh) * nq, nq, 0)
    below = (jnp.arange(n_kb)[:, None] < jnp.arange(n_kb)[None, :]).astype(i32)
    pos = jnp.sum(rows[:, :, None] * below[None], axis=1)
    chunks = (jnp.sum(rows, axis=1) + 1) // 2
    upto = (jnp.arange(nq)[:, None] <= jnp.arange(nq)[None, :]).astype(i32)
    end = jnp.sum(chunks[:, None] * upto, axis=0)
    begin = end - chunks
    t_max = nq * ((nb * KEEP + 1) // 2)
    t_max = -(-t_max // UNROLL) * UNROLL
    t = jnp.arange(t_max, dtype=i32)
    slot = (begin[:, None] * 2 + pos).reshape(-1)[:, None]
    kept = (rows.reshape(-1) > 0)[:, None]
    key = jnp.tile(place, nq)[:, None]
    even = kept & (slot == 2 * t[None])
    odd = kept & (slot == 2 * t[None] + 1)
    work = jnp.stack(
        [
            jnp.sum((end[:, None] <= t[None]).astype(i32), axis=0),
            jnp.sum(jnp.where(even, key, 0), axis=0),
            jnp.sum(jnp.where(odd, key, 0), axis=0),
            jnp.sum(odd.astype(i32), axis=0),
            jnp.sum((begin[:, None] == t[None]).astype(i32), axis=0),
        ]
    )
    turns = (end[-1:] + UNROLL - 1) // UNROLL
    return sel, work, turns


def on_device(nb, nz, tokens, w_query, w_key, w_value, w_out, block_mask):
    me = lax.axis_index("band")
    nh = w_query.shape[1] // HD
    tok_rows = tokens.shape[0]
    nq = tok_rows // BLK
    per = nq // nz
    vmem = pl.BlockSpec(memory_space=pltpu.VMEM)
    smem = pl.BlockSpec(memory_space=pltpu.SMEM)
    hbm = pl.BlockSpec(memory_space=pl.ANY)
    dma = pltpu.SemaphoreType.DMA
    w_full = lax.all_gather(w_out, "head", axis=0, tiled=True)
    sel, work, turns = plan(block_mask, nb, nh, me)
    q_all, kv_all = pl.pallas_call(
        functools.partial(project_exchange, nb, nh),
        out_shape=(
            jax.ShapeDtypeStruct((nh, nq // 2, BLK, BLK), BF16),
            jax.ShapeDtypeStruct((nb * KEEP, BLK, BLK), BF16),
        ),
        in_specs=[smem, vmem, vmem, vmem, vmem],
        out_specs=(hbm, hbm),
        scratch_shapes=[
            pltpu.VMEM((nh, nq // 2, BLK, BLK), BF16),
            pltpu.VMEM((nh, KEEP, BLK, BLK), BF16),
            dma((nb,)),
            dma((nb,)),
            dma((nh,)),
            dma((nh,)),
            dma((2,)),
        ],
        compiler_params=pltpu.CompilerParams(
            collective_id=0, has_side_effects=True, vmem_limit_bytes=32 * MIB
        ),
        name="project_exchange",
    )(sel, tokens.reshape(nq, BLK, -1), w_query, w_key, w_value)
    att = pl.pallas_call(
        attend,
        out_shape=jax.ShapeDtypeStruct((nh * nq + 1, HD, BLK), BF16),
        in_specs=[smem, smem, vmem, vmem],
        out_specs=vmem,
        scratch_shapes=[
            pltpu.VMEM((nh * nq + 1, BLK, BLK), BF16),
            pltpu.VMEM((nb * KEEP, HD, BLK), BF16),
        ],
        compiler_params=pltpu.CompilerParams(vmem_limit_bytes=32 * MIB),
        name="attend",
    )(work, turns, q_all.reshape(nh * nq // 2, BLK, BLK), kv_all)
    n = nh * nz
    return pl.pallas_call(
        functools.partial(exchange_project, nh, nz),
        out_shape=jax.ShapeDtypeStruct((per * BLK, w_out.shape[1]), BF16),
        in_specs=[hbm, vmem],
        out_specs=vmem,
        scratch_shapes=[
            pltpu.VMEM((n, per, HD, BLK), BF16),
            dma((n,)),
            dma((n,)),
            dma((1,)),
        ],
        compiler_params=pltpu.CompilerParams(
            collective_id=1, has_side_effects=True, vmem_limit_bytes=32 * MIB
        ),
        name="exchange_project",
    )(att, w_full)


def solution(mesh):
    return jax.shard_map(
        functools.partial(on_device, mesh.shape["band"], mesh.shape["head"]),
        mesh=mesh,
        in_specs=(
            P(("tiles", "band"), None),
            P(None, "head"),
            P(None, "head"),
            P(None, "head"),
            P("head", None),
            P("tiles", None),
        ),
        out_specs=P(("tiles", "band", "head"), None),
        check_vma=False,
    )
```

```python
import functools
import jax
import jax.numpy as jnp
from jax import lax
from jax.experimental import pallas as pl
from jax.experimental.pallas import tpu as pltpu
from jax.sharding import PartitionSpec as P

HD = 64
BLK = 128
KEEP = 6
UNROLL = 4
LOW = -1e30
SCALE = HD**-0.5 * 1.4426950408889634
MIB = 1 << 20
BF16 = jnp.bfloat16
F32 = jnp.float32
NT = (((1,), (1,)), ((), ()))
TN = (((0,), (0,)), ((), ()))


def greet(peers):
    barrier = pltpu.get_barrier_semaphore()
    for peer in peers:
        pl.semaphore_signal(barrier, inc=1, device_id=peer, device_id_type=pl.DeviceIdType.MESH)


def all_greeted(peers):
    pl.semaphore_wait(pltpu.get_barrier_semaphore(), len(peers))


def make_plan(mask, group, nb, nh, work, turns):
    n_rows, n_kb = mask.shape
    per_band = n_kb // nb
    nq = per_band * nh
    t_max = work.shape[1]
    i32 = jnp.int32
    everything = mask[...].astype(F32)
    rows = mask[pl.ds(group * nq, nq), :].astype(F32)
    named = jnp.max(everything, axis=0, keepdims=True)
    left = lax.broadcasted_iota(i32, (n_kb, n_kb), 0)
    right = lax.broadcasted_iota(i32, (n_kb, n_kb), 1)
    below = (left < right).astype(F32)
    same = (left // per_band == right // per_band).astype(F32)
    rank = jnp.dot(named, below * same, preferred_element_type=F32)
    band = (lax.broadcasted_iota(i32, (1, n_kb), 1) // per_band).astype(F32)
    key = band * KEEP + jnp.minimum(rank, KEEP - 1.0)
    pos = jnp.dot(rows, below, preferred_element_type=F32)
    count = jnp.sum(rows, axis=1, keepdims=True)
    chunks = jnp.floor((count + 1.0) * 0.5)
    qi = lax.broadcasted_iota(i32, (nq, nq), 0)
    qj = lax.broadcasted_iota(i32, (nq, nq), 1)
    begin = jnp.dot(
        (qj < qi).astype(F32), jnp.broadcast_to(chunks, (nq, 128)),
        preferred_element_type=F32, precision=lax.Precision.HIGHEST,
    )[:, :1]
    end = begin + chunks
    slot = jnp.where(rows > 0, begin * 2.0 + pos, -1.0).T
    keys = jnp.broadcast_to(key, (nq, n_kb)).T
    t = lax.broadcasted_iota(i32, (1, t_max), 1).astype(F32)
    first_key = jnp.zeros((n_kb, t_max), F32)
    second_key = jnp.zeros((n_kb, t_max), F32)
    has_second = jnp.zeros((n_kb, t_max), F32)
    for q in range(nq):
        at, value = slot[:, q : q + 1], keys[:, q : q + 1]
        even, odd = at == 2.0 * t, at == 2.0 * t + 1.0
        first_key = first_key + jnp.where(even, value, 0.0)
        second_key = second_key + jnp.where(odd, value, 0.0)
        has_second = has_second + jnp.where(odd, 1.0, 0.0)
    total = lambda x: jnp.sum(x, axis=0, keepdims=True)
    a, b, two = total(first_key), total(second_key), total(has_second)
    work[0:1, :] = total((end <= t).astype(F32)).astype(i32)
    work[1:2, :] = a.astype(i32)
    work[2:3, :] = jnp.where(two > 0, b, a).astype(i32)
    work[3:4, :] = total((begin == t).astype(F32)).astype(i32)
    work[4:5, :] = (1.0 - two).astype(i32)
    work[5:8, :] = jnp.zeros((3, t_max), i32)
    turns[...] = jnp.broadcast_to(
        jnp.floor((jnp.sum(chunks, axis=0, keepdims=True) + (UNROLL - 1.0)) * (1.0 / UNROLL)), (8, 128)
    ).astype(i32)


def select_blocks(mask, me, per_band):
    named = []
    for i in range(per_band):
        named.append(
            functools.reduce(jnp.maximum, [mask[r, me * per_band + i] for r in range(mask.shape[0])])
        )
    picks, rank = [0] * KEEP, 0
    for i in range(per_band):
        for k in range(min(i + 1, KEEP)):
            picks[k] = picks[k] + i * named[i] * (rank == k)
        rank = rank + named[i]
    return picks


def project_exchange(
    nb, nh, mask_s, mask_v, tok_hbm, wq_hbm, wk_hbm, wv_hbm,
    q_all, kv_all, work, turns,
    tok, wq, wk, wv, qs, kvs, send_kv, recv_kv, send_q, recv_q, own, load,
):
    loads = [
        pltpu.make_async_copy(a, b, load.at[i])
        for i, (a, b) in enumerate(((wk_hbm, wk), (wv_hbm, wv), (tok_hbm, tok), (wq_hbm, wq)))
    ]
    for c in loads:
        c.start()
    me = lax.axis_index("band")
    group, place = me // nh, lax.rem(me, nh)
    nq = tok.shape[0]
    others = [lax.rem(me + d, nb) for d in range(1, nb)]
    greet([{"band": p} for p in others])
    sel = select_blocks(mask_s, me, nq)
    for c in loads[:3]:
        c.wait()

    for k in range(KEEP):
        rows = tok[sel[k]]
        keys = jnp.dot(rows, wk[...], preferred_element_type=F32)
        vals = jnp.dot(rows, wv[...], preferred_element_type=F32)
        for h in range(nh):
            cut = slice(h * HD, (h + 1) * HD)
            kvs[h, k] = jnp.concatenate([keys[:, cut], vals[:, cut]], axis=1).astype(BF16)
    all_greeted(others)

    def kv_copy(peer, origin):
        return pltpu.make_async_remote_copy(
            src_ref=kvs.at[lax.rem(peer, nh)],
            dst_ref=kv_all.at[pl.ds(origin * KEEP, KEEP)],
            send_sem=send_kv.at[peer],
            recv_sem=recv_kv.at[origin],
            device_id={"band": peer},
            device_id_type=pl.DeviceIdType.MESH,
        )

    order = [p for _, p in sorted(zip([abs(d - nb // 2) for d in range(1, nb)], range(nb - 1)))]
    for i in order:
        kv_copy(others[i], me).start()
    own_kv = pltpu.make_async_copy(kvs.at[place], kv_all.at[pl.ds(me * KEEP, KEEP)], own.at[0])
    own_kv.start()

    loads[3].wait()
    for m in range(nq // 2):
        two = jnp.dot(
            jnp.concatenate([tok[2 * m], tok[2 * m + 1]], axis=0), wq[...], preferred_element_type=F32
        )
        for h in range(nh):
            cut = slice(h * HD, (h + 1) * HD)
            qs[h, m] = jnp.concatenate([two[:BLK, cut], two[BLK:, cut]], axis=1).astype(BF16)

    def q_copy(to, origin):
        return pltpu.make_async_remote_copy(
            src_ref=qs.at[to],
            dst_ref=q_all.at[origin],
            send_sem=send_q.at[to],
            recv_sem=recv_q.at[origin],
            device_id={"band": group * nh + to},
            device_id_type=pl.DeviceIdType.MESH,
        )

    mates = [lax.rem(place + d, nh) for d in range(1, nh)]
    order_q = [i for _, i in sorted(zip([abs(d - nh // 2) for d in range(1, nh)], range(nh - 1)))]
    for i in order_q:
        q_copy(mates[i], place).start()
    own_q = pltpu.make_async_copy(qs.at[place], q_all.at[place], own.at[1])
    own_q.start()
    make_plan(mask_v, group, nb, nh, work, turns)
    own_kv.wait()
    own_q.wait()
    for p in others:
        kv_copy(p, me).wait_send()
        kv_copy(p, p).wait_recv()
    for p in mates:
        q_copy(p, place).wait_send()
        q_copy(p, p).wait_recv()


def attend(work, turns, q_in, kv, out, q_pad, v_t):
    n_kv, n_pair = kv.shape[0], q_in.shape[0]

    def prepare_kv(c, _):
        v_t[c] = kv[c].T[HD:]
        return 0

    lax.fori_loop(0, n_kv, prepare_kv, 0, unroll=4)
    zeros = jnp.zeros((HD, BLK), BF16)

    def prepare_q(m, _):
        two = q_in[m].T
        q_pad[2 * m] = jnp.concatenate([two[:HD], zeros], axis=0)
        q_pad[2 * m + 1] = jnp.concatenate([two[HD:], zeros], axis=0)
        return 0

    lax.fori_loop(0, n_pair, prepare_q, 0, unroll=2)
    q_pad[2 * n_pair] = jnp.zeros((BLK, BLK), BF16)

    def turn(i, state):
        peak, mass, total = state
        parts = []
        for u in range(UNROLL):
            t = i * UNROLL + u
            q, pair = work[0, t], (work[1, t], work[2, t])
            scores = [jnp.dot(kv[c], q_pad[q], preferred_element_type=F32) * SCALE for c in pair]
            top = functools.reduce(jnp.maximum, [jnp.max(x, axis=0, keepdims=True) for x in scores])
            weights = [jnp.exp2(x - top) for x in scores]
            part = functools.reduce(jnp.add, [jnp.sum(x, axis=0, keepdims=True) for x in weights])
            got = functools.reduce(
                jnp.add,
                [jnp.dot(v_t[c], x.astype(BF16), preferred_element_type=F32) for c, x in zip(pair, weights)],
            )
            parts.append((q, work[3, t], work[4, t], top, part, got))
        for q, first, repeat, top, part, got in parts:
            before = jnp.where(first > 0, LOW, peak)
            peak = jnp.maximum(before, top)
            f = jnp.exp2(before - peak)
            g = jnp.exp2(top - peak) * jnp.where(repeat > 0, 0.5, 1.0)
            mass = mass * f + part * g
            total = total * f + got * g
            out[q] = (total * (1.0 / mass)).astype(BF16)
        return peak, mass, total

    start = (jnp.full((1, BLK), LOW, F32), jnp.zeros((1, BLK), F32), jnp.zeros((HD, BLK), F32))
    lax.fori_loop(0, turns[0, 0], turn, start)


def exchange_project(nh, nz, att, w_hbm, out, got, w_full, send, recv, own):
    band, z = lax.axis_index("band"), lax.axis_index("head")
    group, place = band // nh, lax.rem(band, nh)
    n = nh * nz
    me = z * nh + place
    per = got.shape[1]
    per_band = per * nz
    others = [lax.rem(me + d, n) for d in range(1, n)]
    where = lambda p: {"band": group * nh + lax.rem(p, nh), "head": p // nh}
    w_load = pltpu.make_async_copy(w_hbm, w_full, own.at[1])
    w_load.start()
    greet([where(p) for p in others])
    all_greeted(others)

    def piece(p):
        return att.at[pl.ds(lax.rem(p, nh) * per_band + (p // nh) * per, per)]

    def copy(peer, origin):
        return pltpu.make_async_remote_copy(
            src_ref=piece(peer),
            dst_ref=got.at[origin],
            send_sem=send.at[peer],
            recv_sem=recv.at[origin],
            device_id=where(peer),
            device_id_type=pl.DeviceIdType.MESH,
        )

    for _, i in sorted(zip([abs(d - n // 2) for d in range(1, n)], range(n - 1))):
        copy(others[i], me).start()
    mine = pltpu.make_async_copy(piece(me), got.at[me], own.at[0])
    mine.start()
    mine.wait()
    w_load.wait()
    for p in others:
        copy(p, me).wait_send()
        copy(p, p).wait_recv()
    for r in range(per):
        heads = jnp.concatenate([got[i, r] for i in range(n)], axis=0)
        out[pl.ds(r * BLK, BLK), :] = lax.dot_general(
            heads, w_full[...], TN, preferred_element_type=F32
        ).astype(BF16)


def on_device(nb, nz, tokens, w_query, w_key, w_value, w_out, block_mask):
    nh = w_query.shape[1] // HD
    tok_rows = tokens.shape[0]
    nq = tok_rows // BLK
    per = nq // nz
    vmem = pl.BlockSpec(memory_space=pltpu.VMEM)
    smem = pl.BlockSpec(memory_space=pltpu.SMEM)
    hbm = pl.BlockSpec(memory_space=pl.ANY)
    dma = pltpu.SemaphoreType.DMA
    w_full = lax.all_gather(w_out, "head", axis=0, tiled=True)
    t_max = nh * nq * ((nb * KEEP + 1) // 2)
    t_max = -(-t_max // 128) * 128
    q_all, kv_all, work, turns = pl.pallas_call(
        functools.partial(project_exchange, nb, nh),
        out_shape=(
            jax.ShapeDtypeStruct((nh, nq // 2, BLK, BLK), BF16),
            jax.ShapeDtypeStruct((nb * KEEP, BLK, BLK), BF16),
            jax.ShapeDtypeStruct((8, t_max), jnp.int32),
            jax.ShapeDtypeStruct((8, 128), jnp.int32),
        ),
        in_specs=[smem, vmem, hbm, hbm, hbm, hbm],
        out_specs=(hbm, hbm, vmem, vmem),
        scratch_shapes=[
            pltpu.VMEM((nq, BLK, tokens.shape[1]), BF16),
            pltpu.VMEM(w_query.shape, BF16),
            pltpu.VMEM(w_key.shape, BF16),
            pltpu.VMEM(w_value.shape, BF16),
            pltpu.VMEM((nh, nq // 2, BLK, BLK), BF16),
            pltpu.VMEM((nh, KEEP, BLK, BLK), BF16),
            dma((nb,)),
            dma((nb,)),
            dma((nh,)),
            dma((nh,)),
            dma((2,)),
            dma((4,)),
        ],
        compiler_params=pltpu.CompilerParams(
            collective_id=0, has_side_effects=True, vmem_limit_bytes=32 * MIB
        ),
        name="project_exchange",
    )(block_mask, block_mask, tokens.reshape(nq, BLK, -1), w_query, w_key, w_value)
    att = pl.pallas_call(
        attend,
        out_shape=jax.ShapeDtypeStruct((nh * nq + 1, HD, BLK), BF16),
        in_specs=[smem, smem, vmem, vmem],
        out_specs=vmem,
        scratch_shapes=[
            pltpu.VMEM((nh * nq + 1, BLK, BLK), BF16),
            pltpu.VMEM((nb * KEEP, HD, BLK), BF16),
        ],
        compiler_params=pltpu.CompilerParams(vmem_limit_bytes=32 * MIB),
        name="attend",
    )(work, turns, q_all.reshape(nh * nq // 2, BLK, BLK), kv_all)
    n = nh * nz
    return pl.pallas_call(
        functools.partial(exchange_project, nh, nz),
        out_shape=jax.ShapeDtypeStruct((per * BLK, w_out.shape[1]), BF16),
        in_specs=[hbm, hbm],
        out_specs=vmem,
        scratch_shapes=[
            pltpu.VMEM((n, per, HD, BLK), BF16),
            pltpu.VMEM((w_out.shape[0] * nz, w_out.shape[1]), BF16),
            dma((n,)),
            dma((n,)),
            dma((2,)),
        ],
        compiler_params=pltpu.CompilerParams(
            collective_id=1, has_side_effects=True, vmem_limit_bytes=32 * MIB
        ),
        name="exchange_project",
    )(att, w_full)


def solution(mesh):
    return jax.shard_map(
        functools.partial(on_device, mesh.shape["band"], mesh.shape["head"]),
        mesh=mesh,
        in_specs=(
            P(("tiles", "band"), None),
            P(None, "head"),
            P(None, "head"),
            P(None, "head"),
            P("head", None),
            P("tiles", None),
        ),
        out_specs=P(("tiles", "band", "head"), None),
        check_vma=False,
    )
```

```python
import functools
import jax
import jax.numpy as jnp
from jax import lax
from jax.experimental import pallas as pl
from jax.experimental.pallas import tpu as pltpu
from jax.sharding import PartitionSpec as P

HD = 64
BLK = 128
KEEP = 6
UNROLL = 8
LOW = -1e30
SCALE = HD**-0.5 * 1.4426950408889634
MIB = 1 << 20
BF16 = jnp.bfloat16
F32 = jnp.float32
NT = (((1,), (1,)), ((), ()))
TN = (((0,), (0,)), ((), ()))


def greet(peers):
    barrier = pltpu.get_barrier_semaphore()
    for peer in peers:
        pl.semaphore_signal(barrier, inc=1, device_id=peer, device_id_type=pl.DeviceIdType.MESH)


def all_greeted(peers):
    pl.semaphore_wait(pltpu.get_barrier_semaphore(), len(peers))


def make_plan(mask, group, nb, nh, work, turns):
    n_rows, n_kb = mask.shape
    per_band = n_kb // nb
    nq = per_band * nh
    t_max = work.shape[1]
    i32 = jnp.int32
    everything = mask[...].astype(F32)
    rows = mask[pl.ds(group * nq, nq), :].astype(F32)
    named = jnp.max(everything, axis=0, keepdims=True)
    left = lax.broadcasted_iota(i32, (n_kb, n_kb), 0)
    right = lax.broadcasted_iota(i32, (n_kb, n_kb), 1)
    below = (left < right).astype(F32)
    same = (left // per_band == right // per_band).astype(F32)
    rank = jnp.dot(named, below * same, preferred_element_type=F32)
    band = (lax.broadcasted_iota(i32, (1, n_kb), 1) // per_band).astype(F32)
    key = band * KEEP + jnp.minimum(rank, KEEP - 1.0)
    pos = jnp.dot(rows, below, preferred_element_type=F32)
    count = jnp.sum(rows, axis=1, keepdims=True)
    chunks = jnp.floor((count + 1.0) * 0.5)
    qi = lax.broadcasted_iota(i32, (nq, nq), 0)
    qj = lax.broadcasted_iota(i32, (nq, nq), 1)
    begin = jnp.dot(
        (qj < qi).astype(F32), jnp.broadcast_to(chunks, (nq, 128)),
        preferred_element_type=F32, precision=lax.Precision.HIGHEST,
    )[:, :1]
    end = begin + chunks
    slot = jnp.where(rows > 0, begin * 2.0 + pos, -1.0).T
    keys = jnp.broadcast_to(key, (nq, n_kb)).T
    t = lax.broadcasted_iota(i32, (1, t_max), 1).astype(F32)
    first_key = jnp.zeros((n_kb, t_max), F32)
    second_key = jnp.zeros((n_kb, t_max), F32)
    has_second = jnp.zeros((n_kb, t_max), F32)
    for q in range(nq):
        at, value = slot[:, q : q + 1], keys[:, q : q + 1]
        even, odd = at == 2.0 * t, at == 2.0 * t + 1.0
        first_key = first_key + jnp.where(even, value, 0.0)
        second_key = second_key + jnp.where(odd, value, 0.0)
        has_second = has_second + jnp.where(odd, 1.0, 0.0)
    total = lambda x: jnp.sum(x, axis=0, keepdims=True)
    a, b, two = total(first_key), total(second_key), total(has_second)
    work[0:1, :] = total((end <= t).astype(F32)).astype(i32)
    work[1:2, :] = a.astype(i32)
    work[2:3, :] = jnp.where(two > 0, b, a).astype(i32)
    work[3:4, :] = total((begin == t).astype(F32)).astype(i32)
    work[4:5, :] = (1.0 - two).astype(i32)
    work[5:8, :] = jnp.zeros((3, t_max), i32)
    turns[...] = jnp.broadcast_to(
        jnp.floor((jnp.sum(chunks, axis=0, keepdims=True) + (UNROLL - 1.0)) * (1.0 / UNROLL)), (8, 128)
    ).astype(i32)


def select_blocks(mask, me, per_band):
    named = []
    for i in range(per_band):
        named.append(
            functools.reduce(jnp.maximum, [mask[r, me * per_band + i] for r in range(mask.shape[0])])
        )
    picks, rank = [0] * KEEP, 0
    for i in range(per_band):
        for k in range(min(i + 1, KEEP)):
            picks[k] = picks[k] + i * named[i] * (rank == k)
        rank = rank + named[i]
    return picks


def project_exchange(
    nb, nh, mask_s, mask_v, tok_hbm, wq_hbm, wk_hbm, wv_hbm,
    q_all, kv_all, work, turns,
    tok, wq, wk, wv, qs, kvs, send_kv, recv_kv, send_q, recv_q, own, load,
):
    loads = [
        pltpu.make_async_copy(a, b, load.at[i])
        for i, (a, b) in enumerate(((wk_hbm, wk), (wv_hbm, wv), (tok_hbm, tok), (wq_hbm, wq)))
    ]
    for c in loads:
        c.start()
    me = lax.axis_index("band")
    group, place = me // nh, lax.rem(me, nh)
    nq = tok.shape[0]
    others = [lax.rem(me + d, nb) for d in range(1, nb)]
    greet([{"band": p} for p in others])
    sel = select_blocks(mask_s, me, nq)
    for c in loads[:3]:
        c.wait()

    for k in range(KEEP):
        rows = tok[sel[k]]
        keys = jnp.dot(rows, wk[...], preferred_element_type=F32)
        vals = jnp.dot(rows, wv[...], preferred_element_type=F32)
        for h in range(nh):
            cut = slice(h * HD, (h + 1) * HD)
            kvs[h, k] = jnp.concatenate([keys[:, cut], vals[:, cut]], axis=1).astype(BF16)
    all_greeted(others)

    def kv_copy(peer, origin):
        return pltpu.make_async_remote_copy(
            src_ref=kvs.at[lax.rem(peer, nh)],
            dst_ref=kv_all.at[pl.ds(origin * KEEP, KEEP)],
            send_sem=send_kv.at[peer],
            recv_sem=recv_kv.at[origin],
            device_id={"band": peer},
            device_id_type=pl.DeviceIdType.MESH,
        )

    order = [p for _, p in sorted(zip([abs(d - nb // 2) for d in range(1, nb)], range(nb - 1)))]
    for i in order:
        kv_copy(others[i], me).start()
    own_kv = pltpu.make_async_copy(kvs.at[place], kv_all.at[pl.ds(me * KEEP, KEEP)], own.at[0])
    own_kv.start()

    loads[3].wait()
    for m in range(nq // 2):
        two = jnp.dot(
            jnp.concatenate([tok[2 * m], tok[2 * m + 1]], axis=0), wq[...], preferred_element_type=F32
        )
        for h in range(nh):
            cut = slice(h * HD, (h + 1) * HD)
            qs[h, m] = jnp.concatenate([two[:BLK, cut], two[BLK:, cut]], axis=1).astype(BF16)

    def q_copy(to, origin):
        return pltpu.make_async_remote_copy(
            src_ref=qs.at[to],
            dst_ref=q_all.at[origin],
            send_sem=send_q.at[to],
            recv_sem=recv_q.at[origin],
            device_id={"band": group * nh + to},
            device_id_type=pl.DeviceIdType.MESH,
        )

    mates = [lax.rem(place + d, nh) for d in range(1, nh)]
    order_q = [i for _, i in sorted(zip([abs(d - nh // 2) for d in range(1, nh)], range(nh - 1)))]
    for i in order_q:
        q_copy(mates[i], place).start()
    own_q = pltpu.make_async_copy(qs.at[place], q_all.at[place], own.at[1])
    own_q.start()
    make_plan(mask_v, group, nb, nh, work, turns)
    own_kv.wait()
    own_q.wait()
    for p in others:
        kv_copy(p, me).wait_send()
        kv_copy(p, p).wait_recv()
    for p in mates:
        q_copy(p, place).wait_send()
        q_copy(p, p).wait_recv()


def attend(work, turns, q_in, kv, out, q_pad, v_t):
    n_kv, n_pair = kv.shape[0], q_in.shape[0]

    def prepare_kv(c, _):
        v_t[c] = kv[c].T[HD:]
        return 0

    lax.fori_loop(0, n_kv, prepare_kv, 0, unroll=4)
    zeros = jnp.zeros((HD, BLK), BF16)

    def prepare_q(m, _):
        two = q_in[m].T
        q_pad[2 * m] = jnp.concatenate([two[:HD], zeros], axis=0)
        q_pad[2 * m + 1] = jnp.concatenate([two[HD:], zeros], axis=0)
        return 0

    lax.fori_loop(0, n_pair, prepare_q, 0, unroll=2)
    q_pad[2 * n_pair] = jnp.zeros((BLK, BLK), BF16)

    def turn(i, state):
        peak, mass, total = state
        parts = []
        for u in range(UNROLL):
            t = i * UNROLL + u
            q, pair = work[0, t], (work[1, t], work[2, t])
            scores = [jnp.dot(kv[c], q_pad[q], preferred_element_type=F32) * SCALE for c in pair]
            top = functools.reduce(jnp.maximum, [jnp.max(x, axis=0, keepdims=True) for x in scores])
            weights = [jnp.exp2(x - top) for x in scores]
            part = functools.reduce(jnp.add, [jnp.sum(x, axis=0, keepdims=True) for x in weights])
            got = functools.reduce(
                jnp.add,
                [jnp.dot(v_t[c], x.astype(BF16), preferred_element_type=F32) for c, x in zip(pair, weights)],
            )
            parts.append((q, work[3, t], work[4, t], top, part, got))
        for q, first, repeat, top, part, got in parts:
            before = jnp.where(first > 0, LOW, peak)
            peak = jnp.maximum(before, top)
            f = jnp.exp2(before - peak)
            g = jnp.exp2(top - peak) * jnp.where(repeat > 0, 0.5, 1.0)
            mass = mass * f + part * g
            total = total * f + got * g
            out[q] = (total * (1.0 / mass)).astype(BF16)
        return peak, mass, total

    start = (jnp.full((1, BLK), LOW, F32), jnp.zeros((1, BLK), F32), jnp.zeros((HD, BLK), F32))
    lax.fori_loop(0, turns[0, 0], turn, start)


def exchange_project(nh, nz, att, w_hbm, out, got, w_full, send, recv, own):
    band, z = lax.axis_index("band"), lax.axis_index("head")
    group, place = band // nh, lax.rem(band, nh)
    n = nh * nz
    me = z * nh + place
    per = got.shape[1]
    per_band = per * nz
    others = [lax.rem(me + d, n) for d in range(1, n)]
    where = lambda p: {"band": group * nh + lax.rem(p, nh), "head": p // nh}
    w_load = pltpu.make_async_copy(w_hbm, w_full, own.at[1])
    w_load.start()
    greet([where(p) for p in others])
    all_greeted(others)

    def piece(p):
        return att.at[pl.ds(lax.rem(p, nh) * per_band + (p // nh) * per, per)]

    def copy(peer, origin):
        return pltpu.make_async_remote_copy(
            src_ref=piece(peer),
            dst_ref=got.at[origin],
            send_sem=send.at[peer],
            recv_sem=recv.at[origin],
            device_id=where(peer),
            device_id_type=pl.DeviceIdType.MESH,
        )

    for _, i in sorted(zip([abs(d - n // 2) for d in range(1, n)], range(n - 1))):
        copy(others[i], me).start()
    mine = pltpu.make_async_copy(piece(me), got.at[me], own.at[0])
    mine.start()
    mine.wait()
    w_load.wait()
    for p in others:
        copy(p, me).wait_send()
        copy(p, p).wait_recv()
    for r in range(per):
        heads = jnp.concatenate([got[i, r] for i in range(n)], axis=0)
        out[pl.ds(r * BLK, BLK), :] = lax.dot_general(
            heads, w_full[...], TN, preferred_element_type=F32
        ).astype(BF16)


def on_device(nb, nz, tokens, w_query, w_key, w_value, w_out, block_mask):
    nh = w_query.shape[1] // HD
    tok_rows = tokens.shape[0]
    nq = tok_rows // BLK
    per = nq // nz
    vmem = pl.BlockSpec(memory_space=pltpu.VMEM)
    smem = pl.BlockSpec(memory_space=pltpu.SMEM)
    hbm = pl.BlockSpec(memory_space=pl.ANY)
    dma = pltpu.SemaphoreType.DMA
    w_full = lax.all_gather(w_out, "head", axis=0, tiled=True)
    t_max = nh * nq * ((nb * KEEP + 1) // 2)
    t_max = -(-t_max // 128) * 128
    q_all, kv_all, work, turns = pl.pallas_call(
        functools.partial(project_exchange, nb, nh),
        out_shape=(
            jax.ShapeDtypeStruct((nh, nq // 2, BLK, BLK), BF16),
            jax.ShapeDtypeStruct((nb * KEEP, BLK, BLK), BF16),
            jax.ShapeDtypeStruct((8, t_max), jnp.int32),
            jax.ShapeDtypeStruct((8, 128), jnp.int32),
        ),
        in_specs=[smem, vmem, hbm, hbm, hbm, hbm],
        out_specs=(hbm, hbm, vmem, vmem),
        scratch_shapes=[
            pltpu.VMEM((nq, BLK, tokens.shape[1]), BF16),
            pltpu.VMEM(w_query.shape, BF16),
            pltpu.VMEM(w_key.shape, BF16),
            pltpu.VMEM(w_value.shape, BF16),
            pltpu.VMEM((nh, nq // 2, BLK, BLK), BF16),
            pltpu.VMEM((nh, KEEP, BLK, BLK), BF16),
            dma((nb,)),
            dma((nb,)),
            dma((nh,)),
            dma((nh,)),
            dma((2,)),
            dma((4,)),
        ],
        compiler_params=pltpu.CompilerParams(
            collective_id=0, has_side_effects=True, vmem_limit_bytes=32 * MIB
        ),
        name="project_exchange",
    )(block_mask, block_mask, tokens.reshape(nq, BLK, -1), w_query, w_key, w_value)
    att = pl.pallas_call(
        attend,
        out_shape=jax.ShapeDtypeStruct((nh * nq + 1, HD, BLK), BF16),
        in_specs=[smem, smem, vmem, vmem],
        out_specs=vmem,
        scratch_shapes=[
            pltpu.VMEM((nh * nq + 1, BLK, BLK), BF16),
            pltpu.VMEM((nb * KEEP, HD, BLK), BF16),
        ],
        compiler_params=pltpu.CompilerParams(vmem_limit_bytes=32 * MIB),
        name="attend",
    )(work, turns, q_all.reshape(nh * nq // 2, BLK, BLK), kv_all)
    n = nh * nz
    return pl.pallas_call(
        functools.partial(exchange_project, nh, nz),
        out_shape=jax.ShapeDtypeStruct((per * BLK, w_out.shape[1]), BF16),
        in_specs=[hbm, hbm],
        out_specs=vmem,
        scratch_shapes=[
            pltpu.VMEM((n, per, HD, BLK), BF16),
            pltpu.VMEM((w_out.shape[0] * nz, w_out.shape[1]), BF16),
            dma((n,)),
            dma((n,)),
            dma((2,)),
        ],
        compiler_params=pltpu.CompilerParams(
            collective_id=1, has_side_effects=True, vmem_limit_bytes=32 * MIB
        ),
        name="exchange_project",
    )(att, w_full)


def solution(mesh):
    return jax.shard_map(
        functools.partial(on_device, mesh.shape["band"], mesh.shape["head"]),
        mesh=mesh,
        in_specs=(
            P(("tiles", "band"), None),
            P(None, "head"),
            P(None, "head"),
            P(None, "head"),
            P("head", None),
            P("tiles", None),
        ),
        out_specs=P(("tiles", "band", "head"), None),
        check_vma=False,
    )
```
